128 devices in a mesh: group: 4 (over y), vocab: 32 (over x, z, core).
Axes of the slice: x: 4, y: 4, z: 4, core: 2. Of those that a mesh axis runs over, the one named last changes fastest.
Arguments:
- hidden: bfloat16 [1024, 7168], P('group', 'vocab'), may hold values from -160 to 160
- main_gain: float32 [7168], replicated, may hold values from 0.1 to 1.9
- head_weight: bfloat16 [7168, 65536], P('group', 'vocab'), may hold values from -1 to 1
- token_owner: int32 [32, 4, 8, 1], P('vocab'), may hold values from 0 to 31; in each aligned block of 32 rows (0 to 31, 32 to 63, ..., all dimensions but the last counted through in order) at most 4 rows name the same one
- token_offset: int32 [32, 4, 8, 1], P('vocab'), may hold values from 0 to 2047
- embed_table: bfloat16 [65536, 7168], P('vocab', 'group'), may hold values from -6 to 6
- hidden_gain: float32 [7168], replicated, may hold values from 0.1 to 1.9
- embed_gain: float32 [7168], replicated, may hold values from 0.1 to 1.9
- hidden_projection: bfloat16 [7168, 7168], P('vocab'), may hold values from -1 to 1
- embed_projection: bfloat16 [7168, 7168], P('vocab'), may hold values from -0.046875 to 0.046875
- draft_gain: float32 [7168], replicated, may hold values from 0.1 to 1.9
Outputs:
- main_logprob: bfloat16 [1024, 65536], P('group', 'vocab')
- draft_logprob: bfloat16 [1024, 65536], P('group', 'vocab')
The draws below stay inside these ranges and needn't reach their ends.
Inputs may be any that keep to these rules, and one draw needn't show every extreme that they name: `token_owner`: within the rows of one device (aligned blocks of 32 rows taken in order over the first three dimensions) no shard is named more than 4 times, a bound that some block reaches.
All inputs are finite; a program needn't handle non-finite values.
Results may differ from the reference program's by a relative error of at most 0.0035.
Values may be sent and summed in bfloat16 or wider, within the bound.
No kernel may reach another device: no remote copies, remote signals or barrier semaphores. Data moves between devices by JAX's collectives and lax.ppermute only.
A program may use at most 128 MiB of HBM per device.

```python
import math
import jax
import jax.numpy as jnp
import numpy as np
from jax import lax

D = 7168
VOC_DEV = 2048
ROW_GRP = 256
ROWS = 1024
VOCAB = 65536
LOOK = 32
CAP = 4
N_GROUP = 4
N_VOCAB = 32


def draw_hidden(key, part):
    key = jax.random.fold_in(key, 11)
    key_list = jax.random.split(key, 3)
    row_scale = jnp.exp(jax.random.uniform(key_list[0], (ROWS, 1), minval=0.0, maxval=math.log(10.0)))
    column_scale = jnp.exp(jax.random.uniform(key_list[1], (1, D), minval=0.0, maxval=math.log(4.0)))
    base_values = jnp.clip(jax.random.normal(key_list[2], (ROWS, D)), -4.0, 4.0)
    values = base_values * row_scale * column_scale
    return values.astype(jnp.bfloat16)


def draw_head_weight(key, part):
    key = jax.random.fold_in(key, 23)
    key_list = jax.random.split(key, 1)
    scale_factor = 3.0 / math.sqrt(D)
    values = jnp.clip(jax.random.normal(key_list[0], (D, VOCAB)), -4.0, 4.0) * scale_factor
    return values.astype(jnp.bfloat16)


def draw_hidden_projection(key, part):
    key = jax.random.fold_in(key, 37)
    scale_factor = 1.0 / math.sqrt(2 * D)
    values = jnp.clip(jax.random.normal(key, (D, D)), -4.0, 4.0) * scale_factor
    return values.astype(jnp.bfloat16)


def set_ends(drawn, own_key, smallest, largest):
    place = [jax.random.randint(jax.random.fold_in(own_key, axis), (), 0, length) for axis, length in enumerate(drawn.shape)]
    longest = drawn.shape.index(max(drawn.shape))
    beside = place[:longest] + [(place[longest] + 1) % drawn.shape[longest]] + place[longest + 1:]
    return drawn.at[tuple(place)].set(smallest).at[tuple(beside)].set(largest)


def steps_of(key, extent, pieces, least, largest):
    level, own = 1.0, jax.random.fold_in(key, 6)
    for dim, blocks in pieces:
        steps = jnp.exp(jax.random.uniform(jax.random.fold_in(own, dim), (blocks,), jnp.float32, least / len(pieces), largest / len(pieces)))
        level = level * jnp.repeat(steps, extent[dim] // blocks).reshape([-1 if axis == dim else 1 for axis in range(len(extent))])
    return level


def routed_block(rng, own, number, rows, number_of, top, reach, skew):
    order = jax.random.permutation(rng, number_of)
    heavy_load, common = load_shares(number_of, rows * top, reach, skew, True), load_shares(number_of, rows * top, reach, skew, False)
    places = jnp.arange(number_of)

    def named(lengths, offset_by):
        used = int((lengths > 0).sum())
        fixed = max(1, used // 4)
        shifted = fixed + (places - fixed + offset_by * (used - fixed)) % max(1, number_of - fixed)
        return jnp.zeros((number_of,), jnp.int32).at[order[jnp.where(places < fixed, places, shifted)]].set(jnp.asarray(lengths, jnp.int32))

    lengths = jnp.where(number % 4 == 0, named(heavy_load, number // 4), named(common, number - number // 4 - 1))
    mixed = jax.random.permutation(jax.random.fold_in(own, 3), number_of)
    donor, receiver = mixed[0:number_of // 2 * 2:2], mixed[1:number_of // 2 * 2:2]
    slack = jnp.minimum(lengths[donor] - 1, reach - lengths[receiver]) // 2
    slack = jnp.where((donor == order[0]) | (receiver == order[0]) | (lengths[receiver] == 0), 0, jnp.maximum(slack, 0))
    shifted = jax.random.randint(jax.random.fold_in(own, 4), (number_of // 2,), 0, 1 << 20) % (slack + 1)
    lengths = lengths.at[donor].add(-shifted).at[receiver].add(shifted)
    labels = jnp.searchsorted(jnp.cumsum(lengths), jnp.arange(rows * top), side="right").astype(jnp.int32)
    table = labels.reshape(top, rows).T
    table = table[jax.random.permutation(jax.random.fold_in(own, 1), rows)]
    offset_by = jax.random.randint(jax.random.fold_in(own, 2), (rows, 1), 0, top)
    return jnp.take_along_axis(table, (jnp.arange(top)[None, :] + offset_by) % top, axis=1)


def load_shares(amount, total, reach, slope, full):
    loads = [(1 << 20) // math.isqrt(rank ** slope) + 1 for rank in range(1, amount + 1)]
    largest = reach if full else min(reach, max(-(-total // amount), total * loads[0] // sum(loads)))
    least = 1 if total - largest >= amount - 1 else 0
    holding, rest = [largest] + [least] * (amount - 1), total - largest - least * (amount - 1)
    while rest > 0:
        movable = [i for i in range(1, amount) if holding[i] < largest] or [i for i in range(1, amount) if holding[i] < reach]
        mass, left = sum([loads[i] for i in movable]), rest
        for i in movable:
            more = min(reach - holding[i], max(1, left * loads[i] // mass), rest)
            holding[i] = holding[i] + more
            rest = rest - more
    return np.array(holding)


def scatter_about(rng, extent, scale, limit, pieces=(), kind=jnp.bfloat16):
    result = jax.random.normal(rng, extent, jnp.float32) * scale
    if len(pieces) > 0:
        result = steps_of(rng, extent, pieces, -0.22, 0.18) * result
    return jnp.clip(result, min=-limit, max=limit).astype(kind)


def setup_inputs(seed: int = 0) -> dict:
    splits = jax.random.split(jax.random.key(seed), 12)
    hidden = draw_hidden(jax.random.fold_in(splits[11], 71), 0)
    main_gain = jnp.clip(1.0 + 0.18 * jax.random.normal(splits[1], (D,), jnp.float32), 0.1, 1.9)
    head_weight = draw_head_weight(jax.random.fold_in(splits[11], 71), 0)
    token_owner_keys = jax.random.split(jax.random.fold_in(splits[3], 1), N_VOCAB * N_GROUP * (ROW_GRP // N_VOCAB) // LOOK)
    token_owner_turns = jax.random.permutation(jax.random.fold_in(splits[3], 3), N_VOCAB * N_GROUP * (ROW_GRP // N_VOCAB) // LOOK)
    token_owner = jax.vmap(lambda own, number: routed_block(jax.random.fold_in(splits[3], 2), own, number, LOOK, N_VOCAB, 1, CAP, 2))(token_owner_keys, token_owner_turns).reshape((N_VOCAB, N_GROUP, ROW_GRP // N_VOCAB, 1))
    token_offset = set_ends(jax.random.randint(splits[4], (N_VOCAB, N_GROUP, ROW_GRP // N_VOCAB, 1), 0, VOC_DEV), jax.random.fold_in(splits[4], 1), 0, VOC_DEV - 1).astype(jnp.int32)
    embed_table = scatter_about(splits[5], (VOCAB, D), 1.0, 6.0, ((0, 32), (1, 4)))
    hidden_gain = jnp.clip(1.0 + 0.18 * jax.random.normal(splits[6], (D,), jnp.float32), 0.1, 1.9)
    embed_gain = jnp.clip(1.0 + 0.18 * jax.random.normal(splits[7], (D,), jnp.float32), 0.1, 1.9)
    hidden_projection = draw_hidden_projection(jax.random.fold_in(splits[11], 71), 0)
    embed_projection = scatter_about(splits[9], (D, D), (2 * D) ** -0.5, 0.046875, ((0, 32),))
    draft_gain = jnp.clip(1.0 + 0.18 * jax.random.normal(splits[10], (D,), jnp.float32), 0.1, 1.9)
    return dict(hidden=hidden, main_gain=main_gain, head_weight=head_weight, token_owner=token_owner, token_offset=token_offset, embed_table=embed_table, hidden_gain=hidden_gain, embed_gain=embed_gain, hidden_projection=hidden_projection, embed_projection=embed_projection, draft_gain=draft_gain)


def normed(values, gain):
    square_mean = lax.optimization_barrier(jnp.mean(values * values, axis=-1, keepdims=True))
    return values * lax.rsqrt(square_mean + 1e-06) * gain

def reference(hidden, main_gain, head_weight, token_owner, token_offset, embed_table, hidden_gain, embed_gain, hidden_projection, embed_projection, draft_gain):
    hidden_values = hidden.astype(jnp.float32)
    main_input = normed(hidden_values, main_gain).astype(jnp.bfloat16)
    main_scores = jnp.dot(main_input, head_weight, preferred_element_type=jnp.float32)
    main_logprob = jax.nn.log_softmax(main_scores, axis=-1).astype(jnp.bfloat16)
    owners = jnp.transpose(token_owner, (1, 0, 2, 3)).reshape(-1).astype(jnp.int32)
    offsets = jnp.transpose(token_offset, (1, 0, 2, 3)).reshape(-1).astype(jnp.int32)
    next_token = owners * VOC_DEV + offsets
    embed_rows = jnp.take(embed_table, next_token, axis=0).astype(jnp.float32)
    embed_input = normed(embed_rows, embed_gain).astype(jnp.bfloat16)
    draft_hidden = normed(hidden_values, hidden_gain).astype(jnp.bfloat16)
    state_total = jnp.dot(draft_hidden, hidden_projection, preferred_element_type=jnp.float32) + jnp.dot(embed_input, embed_projection, preferred_element_type=jnp.float32)
    draft_input = normed(state_total, draft_gain).astype(jnp.bfloat16)
    draft_scores = jnp.dot(draft_input, head_weight, preferred_element_type=jnp.float32)
    draft_logprob = jax.nn.log_softmax(draft_scores, axis=-1).astype(jnp.bfloat16)
    return (main_logprob, draft_logprob)
```

```python
import jax
import jax.numpy as jnp
from jax import lax
from jax.sharding import Mesh, PartitionSpec as P

epsilon = 1e-06
bf16 = jnp.bfloat16
f32 = jnp.float32
VOCAB_AXES = ("x", "z", "core")
SIDE = 4


def shift_pairs(step):
    return [(place, (place + step) % SIDE) for place in range(SIDE)]


def dot(left, right):
    return jnp.dot(left, right, preferred_element_type=f32)


def swap_core(value):
    return lax.ppermute(value, "core", [(0, 1), (1, 0)])


def transpose_plane(value):
    pairs = [(a * SIDE + b, b * SIDE + a) for a in range(SIDE) for b in range(SIDE)]
    return lax.ppermute(value, ("group", "x"), pairs)


def piece_at(value, place, dimension):
    size = value.shape[dimension] // SIDE
    return lax.dynamic_slice_in_dim(value, place * size, size, dimension)


def scatter_sum(value, axis, dimension):
    place = lax.axis_index(axis)
    total = piece_at(value, place, dimension).astype(f32)
    for step in (1, 3, 2):
        sent = piece_at(value, (place + step) % SIDE, dimension).astype(bf16)
        total = total + lax.ppermute(sent, axis, shift_pairs(step)).astype(f32)
    return total


def gather_along(value, axis, dimension):
    place = lax.axis_index(axis)
    from_step = {step: lax.ppermute(value, axis, shift_pairs(step)) for step in (1, 3, 2)}
    ordered = [from_step[3], from_step[2], from_step[1], value, from_step[3], from_step[2], from_step[1]]
    size = value.shape[dimension]
    stacked = jnp.concatenate(ordered, axis=dimension)
    return lax.dynamic_slice_in_dim(stacked, (3 - place) * size, SIDE * size, dimension)


def gather_small(value):
    copies = jnp.broadcast_to(value[None], (32,) + value.shape)
    return lax.all_to_all(copies, VOCAB_AXES, split_axis=0, concat_axis=0, tiled=True)


def log_sums(scores):
    peak = jnp.max(scores, axis=1)
    total = jnp.sum(jnp.exp(scores - peak[:, None]), axis=1)
    every = gather_small(jnp.concatenate([peak, total]))
    rows = scores.shape[0]
    peaks, totals = every[:, :rows], every[:, rows:]
    top = jnp.max(peaks, axis=0)
    return top + jnp.log(jnp.sum(totals * jnp.exp(peaks - top[None]), axis=0))


def per_device(
    hidden,
    main_gain,
    head_weight,
    token_owner,
    token_offset,
    embed_table,
    hidden_gain,
    embed_gain,
    hidden_projection,
    embed_projection,
    draft_gain,
):
    group = lax.axis_index("group")
    x_place = lax.axis_index("x")
    z_place = lax.axis_index("z")
    core = lax.axis_index("core")
    vocab = (x_place * SIDE + z_place) * 2 + core
    rows, slice_width = hidden.shape
    full_width = main_gain.shape[0]
    quarter = full_width // SIDE

    hidden_values = hidden.astype(f32)

    main_slice = lax.dynamic_slice_in_dim(main_gain, vocab * slice_width, slice_width, 0)
    main_piece = (hidden_values * main_slice).astype(bf16).T
    main_moved = transpose_plane(main_piece)
    main_stack = lax.all_gather(main_moved, VOCAB_AXES, axis=0, tiled=True).reshape(
        SIDE, quarter, rows
    )

    squares = gather_small(jnp.sum(hidden_values * hidden_values, axis=1))
    hidden_scale = lax.rsqrt(jnp.sum(squares, axis=0) / full_width + epsilon)

    owners = token_owner.reshape(-1)
    offsets = token_offset.reshape(-1)
    look = owners.shape[0]
    shards = 32
    capacity = 4
    tokens = gather_small(owners * 2048 + offsets)
    wanted = (tokens // 2048) == vocab
    rank = jnp.cumsum(wanted.astype(jnp.int32), axis=1) - 1
    slot = jnp.arange(capacity, dtype=jnp.int32)
    chosen = wanted[:, None, :] & (rank[:, None, :] == slot[None, :, None])
    requests = jnp.sum(jnp.where(chosen, (tokens % 2048)[:, None, :], 0), axis=2).reshape(-1)
    table_rows = embed_table.shape[0]
    pick = (requests[:, None] == jnp.arange(table_rows, dtype=jnp.int32)[None, :]).astype(bf16)
    found = dot(pick, embed_table).astype(bf16)
    returned = lax.all_to_all(
        found.reshape(shards, capacity, quarter), VOCAB_AXES, split_axis=0, concat_axis=0, tiled=True
    ).reshape(shards * capacity, quarter)
    matches = owners[:, None] == jnp.arange(shards, dtype=jnp.int32)[None, :]
    earlier = jnp.cumsum(matches.astype(jnp.int32), axis=0) - 1
    own_rank = jnp.sum(jnp.where(matches, earlier, 0), axis=1)
    place = owners * capacity + own_rank
    put = (place[:, None] == jnp.arange(shards * capacity, dtype=jnp.int32)[None, :]).astype(bf16)
    fetched = dot(put, returned).astype(bf16)
    quarters = lax.all_to_all(
        fetched.reshape(SIDE, look // SIDE, quarter), "group", split_axis=0, concat_axis=0, tiled=True
    )
    embed_rows = quarters.astype(f32)
    embed_squares = jnp.sum(embed_rows * embed_rows, axis=(0, 2), keepdims=True)
    embed_input = (
        embed_rows
        * lax.rsqrt(embed_squares / full_width + epsilon)
        * embed_gain.reshape(SIDE, 1, quarter)
    ).astype(bf16)
    send = embed_input.reshape(SIDE, look // SIDE, shards // SIDE, slice_width)
    send = send.transpose(0, 2, 1, 3).reshape(shards, look // SIDE, slice_width)
    embed_slice = lax.all_to_all(
        send, VOCAB_AXES, split_axis=0, concat_axis=0, tiled=True
    ).reshape(rows, slice_width)

    hidden_slice = lax.dynamic_slice_in_dim(hidden_gain, vocab * slice_width, slice_width, 0)
    draft_hidden = (hidden_values * hidden_scale[:, None] * hidden_slice).astype(bf16)

    half = rows // 2
    quarter_gain = lax.dynamic_slice_in_dim(draft_gain, x_place * quarter, quarter, 0)
    state_pieces = []
    for part in range(2):
        cut = slice(part * half, (part + 1) * half)
        terms = dot(draft_hidden[cut], hidden_projection) + dot(embed_slice[cut], embed_projection)
        terms = terms.reshape(2, half // 2, full_width)
        other = lax.dynamic_index_in_dim(terms, 1 - core, 0, keepdims=False).astype(bf16)
        own = lax.dynamic_index_in_dim(terms, core, 0, keepdims=False)
        pair = own + swap_core(other).astype(f32)
        if part == 0:
            state = scatter_sum(scatter_sum(pair, "x", 1), "z", 0)
        else:
            state = scatter_sum(scatter_sum(pair, "z", 0), "x", 1)
        state_pieces.append(state)
    state_both = jnp.stack(state_pieces)
    state_squares = jnp.sum(state_both * state_both, axis=2)
    draft_piece = (state_both * quarter_gain).astype(bf16)
    draft_moved = transpose_plane(draft_piece)
    first = gather_along(gather_along(draft_moved[0], "z", 0)[None], "x", 0)
    second = gather_along(gather_along(draft_moved[1][None], "x", 0), "z", 1)
    mine = jnp.stack([first, second])
    theirs = swap_core(mine)
    lower = jnp.where(core == 0, mine, theirs)
    upper = jnp.where(core == 0, theirs, mine)
    draft_stack = jnp.concatenate([lower, upper], axis=2)

    all_squares = gather_small(state_squares.reshape(-1)).reshape(SIDE, SIDE, 2, 2, -1)
    all_squares = jnp.sum(all_squares, axis=0).transpose(2, 1, 0, 3).reshape(-1)
    draft_scale = lax.rsqrt(all_squares / full_width + epsilon)

    main_partial = jnp.einsum(
        "gkr,kn->grn", main_stack, head_weight, preferred_element_type=f32
    ).astype(bf16)
    main_raw = lax.psum_scatter(
        main_partial.reshape(SIDE * rows, -1), "group", scatter_dimension=0, tiled=True
    )
    main_scores = main_raw.astype(f32) * hidden_scale[:, None]
    main_out = (main_scores - log_sums(main_scores)[:, None]).astype(bf16)

    def block(part, step):
        return lax.dynamic_index_in_dim(
            draft_stack[part], (group + step) % SIDE, 0, keepdims=False
        )

    carry = [None, None]
    for hop in range(4):
        steps = [(-1 - hop) % SIDE, (1 + hop) % SIDE]
        left = jnp.concatenate([block(0, steps[0]), block(1, steps[1])])
        terms = dot(left, head_weight)
        terms = [terms[:half], terms[half:]]
        for part in range(2):
            total = terms[part]
            if hop > 0:
                total = total + carry[part].astype(f32)
            if hop < 3:
                total = lax.ppermute(total.astype(bf16), "group", shift_pairs(1 if part == 0 else 3))
            carry[part] = total
    draft_scores = jnp.concatenate(carry) * draft_scale[:, None]
    draft_out = (draft_scores - log_sums(draft_scores)[:, None]).astype(bf16)
    return main_out, draft_out


def solution(mesh):
    vocab = mesh.shape["vocab"]
    whole = Mesh(
        mesh.devices.reshape(SIDE, SIDE, vocab // SIDE // 2, 2), ("group", "x", "z", "core")
    )
    placed = (
        P("group", VOCAB_AXES),
        P(),
        P("group", VOCAB_AXES),
        P(VOCAB_AXES, None, None, None),
        P(VOCAB_AXES, None, None, None),
        P(VOCAB_AXES, "group"),
        P(),
        P(),
        P(VOCAB_AXES, None),
        P(VOCAB_AXES, None),
        P(),
    )
    return jax.shard_map(
        per_device,
        mesh=whole,
        in_specs=placed,
        out_specs=(P("group", VOCAB_AXES), P("group", VOCAB_AXES)),
        check_vma=False,
    )
```

```python
import functools

import jax
import jax.numpy as jnp
from jax import lax
from jax.experimental import pallas as pl
from jax.experimental.pallas import tpu as pltpu
from jax.sharding import Mesh, PartitionSpec as P

epsilon = 1e-06
bf16 = jnp.bfloat16
f32 = jnp.float32
VOCAB_AXES = ("x", "z", "core")
SIDE = 4


def shift_pairs(step):
    return [(place, (place + step) % SIDE) for place in range(SIDE)]


def dot(left, right):
    return jnp.dot(left, right, preferred_element_type=f32)


def swap_core(value):
    return lax.ppermute(value, "core", [(0, 1), (1, 0)])


def transpose_plane(value):
    pairs = [(a * SIDE + b, b * SIDE + a) for a in range(SIDE) for b in range(SIDE)]
    return lax.ppermute(value, ("group", "x"), pairs)


def piece_at(value, place, dimension):
    size = value.shape[dimension] // SIDE
    return lax.dynamic_slice_in_dim(value, place * size, size, dimension)


def scatter_sum(value, axis, dimension):
    place = lax.axis_index(axis)
    total = piece_at(value, place, dimension).astype(f32)
    for step in (1, 3, 2):
        sent = piece_at(value, (place + step) % SIDE, dimension).astype(bf16)
        total = total + lax.ppermute(sent, axis, shift_pairs(step)).astype(f32)
    return total


def exchange(value, axis, dimension):
    place = lax.axis_index(axis)
    moved = [piece_at(value, place, dimension)]
    for step in (1, 2, 3):
        sent = piece_at(value, (place + step) % SIDE, dimension)
        moved.append(lax.ppermute(sent, axis, shift_pairs(step)))
    return moved


def in_order(moved, axis, dimension):
    place = lax.axis_index(axis)
    size = moved[0].shape[dimension]
    ordered = [moved[3], moved[2], moved[1], moved[0], moved[3], moved[2], moved[1]]
    stacked = jnp.concatenate(ordered, axis=dimension)
    return lax.dynamic_slice_in_dim(stacked, (3 - place) * size, SIDE * size, dimension)


def gather_along(value, axis, dimension):
    moved = [value] + [lax.ppermute(value, axis, shift_pairs(step)) for step in (1, 2, 3)]
    return in_order(moved, axis, dimension)


def gather_small(value):
    copies = jnp.broadcast_to(value[None], (32,) + value.shape)
    return lax.all_to_all(copies, VOCAB_AXES, split_axis=0, concat_axis=0, tiled=True)


def peak_and_sum(scores):
    peak = jnp.max(scores, axis=1)
    return peak, jnp.sum(jnp.exp(scores - peak[:, None]), axis=1)


def log_sums(peaks, totals):
    top = jnp.max(peaks, axis=0)
    return top + jnp.log(jnp.sum(totals * jnp.exp(peaks - top[None]), axis=0))


def crossed_pairs(step, turn):
    pairs = []
    for x in range(SIDE):
        for z in range(SIDE):
            for core in range(2):
                to_x, to_z = (x + step) % SIDE, (z + step) % SIDE
                target = (to_x, z) if core == turn else (x, to_z)
                pairs.append(((x * SIDE + z) * 2 + core, (target[0] * SIDE + target[1]) * 2 + core))
    return pairs


def crossed(value, step, turn):
    return lax.ppermute(value, VOCAB_AXES, crossed_pairs(step, turn))


def by_core(mine, core):
    theirs = swap_core(mine)
    return jnp.where(core == 0, mine, theirs), jnp.where(core == 0, theirs, mine)


def assemble_kernel(first_hop, places, gain, *refs):
    mine, theirs = refs[:SIDE], refs[SIDE : 2 * SIDE]
    out, squares, held = refs[2 * SIDE :]
    group, core = places[0], places[3]
    block_rows = held.shape[0]
    slab = block_rows // 2

    def one(index, _):
        number, quarter = index // SIDE, lax.rem(index, SIDE)
        hop = number + first_hop
        block = lax.rem(jnp.where(quarter < 2, group - 1 - hop, group + 1 + hop) + 2 * SIDE, SIDE)
        owner = block // 2
        lower = lax.rem(block, 2) == 0
        place = jnp.where(owner == 0, places[1], places[2])
        source = lax.rem(place - quarter + SIDE, SIDE)
        for step in range(SIDE):
            for own, pieces in ((True, mine), (False, theirs)):

                @pl.when((source == step) & ((owner == core) == own))
                def _(ref=pieces[step]):
                    held[...] = ref[...]

        for part in range(slab // 16):
            values = held[part * 32 : (part + 1) * 32, :].astype(f32)
            even = jnp.concatenate([values[0:8], values[16:24]])
            odd = jnp.concatenate([values[8:16], values[24:32]])
            chosen = jnp.where(lower, even, odd)
            rows = pl.ds(pl.multiple_of(quarter * slab + part * 16, 16), 16)
            squares[number, rows, :] = jnp.sum(chosen * chosen, axis=1, keepdims=True)
            out[number, rows, :] = (chosen * gain[...]).astype(bf16)
        return 0

    lax.fori_loop(0, out.shape[0] * SIDE, one, 0)


def assemble(first_hop, count, places, gain, mine, theirs, rows):
    width = gain.shape[0]
    vmem = pl.BlockSpec(memory_space=pltpu.VMEM)
    return pl.pallas_call(
        functools.partial(assemble_kernel, first_hop),
        out_shape=(
            jax.ShapeDtypeStruct((count, rows, width), bf16),
            jax.ShapeDtypeStruct((count, rows, 1), f32),
        ),
        in_specs=[pl.BlockSpec(memory_space=pltpu.SMEM)] + [vmem] * (1 + 2 * SIDE),
        out_specs=(vmem, vmem),
        scratch_shapes=[pltpu.VMEM((rows // 2, width), bf16)],
        compiler_params=pltpu.CompilerParams(vmem_limit_bytes=24 * 1024 * 1024),
        cost_estimate=pl.CostEstimate(
            flops=count * rows * width * 4, bytes_accessed=count * rows * width * 4, transcendentals=0
        ),
    )(places, gain.reshape(1, width), *mine, *theirs)


def embed_kernel(full_width, places, gain, *refs):
    pieces, out = refs[:SIDE], refs[SIDE]
    values = [piece[...].astype(f32) for piece in pieces]
    total = sum(jnp.sum(value * value, axis=1, keepdims=True) for value in values)
    scale = lax.rsqrt(total / full_width + epsilon)
    pair_rows, pair_width = out.shape[1:]
    for step in range(SIDE):
        place = lax.rem(places[0] - step + SIDE, SIDE)
        normed = (values[step] * scale * gain[place]).astype(bf16)
        for z in range(SIDE):
            for core in range(2):
                out[place * 2 * SIDE + z * 2 + core] = normed[
                    core * pair_rows : (core + 1) * pair_rows, z * pair_width : (z + 1) * pair_width
                ]


def embed_slices(places, gain, pieces, full_width, shards):
    look, quarter = pieces[0].shape
    vmem = pl.BlockSpec(memory_space=pltpu.VMEM)
    return pl.pallas_call(
        functools.partial(embed_kernel, full_width),
        out_shape=jax.ShapeDtypeStruct((shards, look // 2, quarter // SIDE), bf16),
        in_specs=[pl.BlockSpec(memory_space=pltpu.SMEM)] + [vmem] * (1 + SIDE),
        out_specs=vmem,
        compiler_params=pltpu.CompilerParams(vmem_limit_bytes=16 * 1024 * 1024),
        cost_estimate=pl.CostEstimate(
            flops=look * full_width * 4, bytes_accessed=look * full_width * 4, transcendentals=0
        ),
    )(places, gain.reshape(SIDE, 1, quarter), *pieces)


def per_device(
    hidden,
    main_gain,
    head_weight,
    token_owner,
    token_offset,
    embed_table,
    hidden_gain,
    embed_gain,
    hidden_projection,
    embed_projection,
    draft_gain,
):
    group = lax.axis_index("group")
    x_place = lax.axis_index("x")
    z_place = lax.axis_index("z")
    core = lax.axis_index("core")
    vocab = (x_place * SIDE + z_place) * 2 + core
    rows, slice_width = hidden.shape
    full_width = main_gain.shape[0]
    quarter = full_width // SIDE

    hidden_values = hidden.astype(f32)

    places = jnp.stack([group, x_place, z_place, core]).astype(jnp.int32)

    main_slice = lax.dynamic_slice_in_dim(main_gain, vocab * slice_width, slice_width, 0)
    main_piece = (hidden_values * main_slice).astype(bf16).T
    main_moved = transpose_plane(main_piece)

    hidden_slice = lax.dynamic_slice_in_dim(hidden_gain, vocab * slice_width, slice_width, 0)
    hidden_piece = (hidden_values * hidden_slice).astype(bf16)
    hidden_moved = [hidden_piece]
    hidden_moved += [lax.ppermute(hidden_piece, "group", shift_pairs(step)) for step in (1, 2, 3)]

    shards = 32
    capacity = 4
    owner_block = token_owner.astype(f32)
    token_block = (owner_block * 2048.0 + token_offset.astype(f32)).reshape(-1)
    look = token_block.shape[0]
    squares = jnp.sum(hidden_values * hidden_values, axis=1)
    gathered = gather_small(jnp.concatenate([token_block, squares]))
    gathered, main_moved, hidden_moved = lax.optimization_barrier(
        (gathered, main_moved, hidden_moved)
    )
    main_stack = lax.all_gather(main_moved, VOCAB_AXES, axis=0, tiled=True).reshape(
        SIDE, quarter, rows
    )
    hidden_scale = lax.rsqrt(jnp.sum(gathered[:, look:], axis=0) / full_width + epsilon)

    block_rows = rows // shards
    pair_rows = 2 * block_rows
    pair_width = 2 * slice_width

    def both_slices(weight):
        mine = lax.dynamic_slice_in_dim(weight, group * quarter, quarter, 1)
        return jnp.concatenate(by_core(mine, core))

    hidden_weight = both_slices(hidden_projection)
    embed_weight = both_slices(embed_projection)

    hidden_all = jnp.stack(hidden_moved)

    def pair_of(stacked, which):
        taken = [
            lax.dynamic_index_in_dim(stacked, (group - 2 * which - e) % SIDE, 0, keepdims=False)
            for e in range(2)
        ]
        return jnp.stack(taken)

    own = pair_of(hidden_all, core)
    other = swap_core(pair_of(hidden_all, 1 - core))
    hidden_pair = jnp.concatenate(
        [jnp.where(core == 0, own, other), jnp.where(core == 0, other, own)], axis=2
    ).reshape(2, shards, block_rows, pair_width)
    hidden_pair = hidden_pair.transpose(1, 0, 2, 3).reshape(shards * pair_rows, pair_width)
    scales = [hidden_scale]
    scales += [lax.ppermute(hidden_scale, "group", shift_pairs(step)) for step in (1, 2, 3)]
    pair_scale = pair_of(jnp.stack(scales), core).reshape(2, shards, block_rows)
    pair_scale = pair_scale.transpose(1, 0, 2).reshape(shards * pair_rows, 1)
    hidden_terms = dot(hidden_pair, hidden_weight) * pair_scale

    tokens = gathered[:, :look].astype(jnp.int32)
    wanted = (tokens // 2048) == vocab
    rank = jnp.cumsum(wanted.astype(jnp.int32), axis=1) - 1
    slot = jnp.arange(capacity, dtype=jnp.int32)
    chosen = wanted[:, None, :] & (rank[:, None, :] == slot[None, :, None])
    requests = jnp.sum(jnp.where(chosen, (tokens % 2048)[:, None, :], 0), axis=2).reshape(-1)
    table_rows = embed_table.shape[0]
    pick = (requests[:, None] == jnp.arange(table_rows, dtype=jnp.int32)[None, :]).astype(bf16)
    found = dot(pick, embed_table).astype(bf16)
    returned = lax.all_to_all(
        found.reshape(shards, capacity, quarter), VOCAB_AXES, split_axis=0, concat_axis=0, tiled=True
    ).reshape(shards * capacity, quarter)
    returned, hidden_terms, embed_weight = lax.optimization_barrier(
        (returned, hidden_terms, embed_weight)
    )
    owners = lax.dynamic_index_in_dim(tokens, vocab, 0, keepdims=False) // 2048
    matches = owners[:, None] == jnp.arange(shards, dtype=jnp.int32)[None, :]
    earlier = jnp.cumsum(matches.astype(jnp.int32), axis=0) - 1
    own_rank = jnp.sum(jnp.where(matches, earlier, 0), axis=1)
    place = owners * capacity + own_rank
    put = (place[:, None] == jnp.arange(shards * capacity, dtype=jnp.int32)[None, :]).astype(bf16)
    fetched = dot(put, returned).astype(bf16)
    fetched_moved = [fetched]
    fetched_moved += [lax.ppermute(fetched, "group", shift_pairs(step)) for step in (1, 2, 3)]
    send = embed_slices(places, embed_gain, fetched_moved, full_width, shards)
    embed_pair = lax.all_to_all(
        send, VOCAB_AXES, split_axis=0, concat_axis=0, tiled=True
    ).reshape(shards * pair_rows, pair_width)

    main_partial = jnp.einsum(
        "gkr,kn->grn", main_stack, head_weight, preferred_element_type=f32
    ).astype(bf16)
    embed_pair, main_partial = lax.optimization_barrier((embed_pair, main_partial))
    main_raw = lax.psum_scatter(
        main_partial.reshape(SIDE * rows, -1), "group", scatter_dimension=0, tiled=True
    )

    state = hidden_terms + dot(embed_pair, embed_weight)
    state_gain = lax.dynamic_slice_in_dim(draft_gain, group * quarter, quarter, 0)
    outer = jnp.where(core == 0, x_place, z_place)
    total = piece_at(state, outer, 0)
    for step in (2, 1, 3):
        sent = piece_at(state, (outer + step) % SIDE, 0).astype(bf16)
        total = total + crossed(sent, step, 0).astype(f32)
    sent = total.astype(bf16)
    for step in (2, 1, 3):
        total = total + crossed(sent, step, 1).astype(f32)
    sent = total.astype(bf16)
    mine = [sent] + [crossed(sent, step, 0) for step in (1, 2, 3)]
    theirs = [swap_core(piece) for piece in mine]
    put_together = functools.partial(
        assemble, places=places, gain=state_gain, mine=mine, theirs=theirs, rows=rows
    )
    half = rows // 2
    first, first_squares = put_together(0, 1)
    carry = [None, None]
    for hop in range(4):
        if hop == 2:
            carry, first_squares, rest_squares = lax.optimization_barrier(
                (carry, first_squares, rest_squares)
            )
            above, below = [], []
            for rows_squares in (first_squares[0], rest_squares[0], rest_squares[1], rest_squares[2]):
                above.append(rows_squares[:half, 0])
                below.append(rows_squares[half:, 0])
            state_squares = jnp.concatenate([above[3], below[3]])
            for step in (1, 2, 3):
                sent = jnp.concatenate([above[3 - step], below[step - 1]])
                state_squares = state_squares + lax.ppermute(sent, "group", shift_pairs(step))
            draft_scale = lax.rsqrt(state_squares / full_width + epsilon)
        terms = dot(first[0] if hop == 0 else rest[hop - 1], head_weight)
        if hop == 0:
            terms, places_later = lax.optimization_barrier((terms.astype(bf16), places))
            rest, rest_squares = put_together(1, 3, places=places_later)
        if hop == 3:
            main_scores = main_raw.astype(f32) * hidden_scale[:, None]
            main_stats = peak_and_sum(main_scores)
            carry, main_stats, draft_scale = lax.optimization_barrier((carry, main_stats, draft_scale))
        terms = [terms[:half], terms[half:]]
        for part in range(2):
            total = terms[part]
            if hop > 0:
                total = total + carry[part].astype(f32)
            if hop < 3:
                total = lax.ppermute(total.astype(bf16), "group", shift_pairs(1 if part == 0 else 3))
            carry[part] = total
    draft_scores = jnp.concatenate(carry) * draft_scale[:, None]
    stats = jnp.concatenate(main_stats + peak_and_sum(draft_scores))
    every = gather_small(stats).reshape(shards, 4, rows)
    main_out = (main_scores - log_sums(every[:, 0], every[:, 1])[:, None]).astype(bf16)
    draft_out = (draft_scores - log_sums(every[:, 2], every[:, 3])[:, None]).astype(bf16)
    return main_out, draft_out


def solution(mesh):
    vocab = mesh.shape["vocab"]
    whole = Mesh(
        mesh.devices.reshape(SIDE, SIDE, vocab // SIDE // 2, 2), ("group", "x", "z", "core")
    )
    placed = (
        P("group", VOCAB_AXES),
        P(),
        P("group", VOCAB_AXES),
        P(VOCAB_AXES, None, None, None),
        P(VOCAB_AXES, None, None, None),
        P(VOCAB_AXES, "group"),
        P(),
        P(),
        P(VOCAB_AXES, None),
        P(VOCAB_AXES, None),
        P(),
    )
    return jax.shard_map(
        per_device,
        mesh=whole,
        in_specs=placed,
        out_specs=(P("group", VOCAB_AXES), P("group", VOCAB_AXES)),
        check_vma=False,
    )
```

```python
import functools

import jax
import jax.numpy as jnp
from jax import lax
from jax.experimental import pallas as pl
from jax.experimental.pallas import tpu as pltpu
from jax.sharding import Mesh, PartitionSpec as P

epsilon = 1e-06
bf16 = jnp.bfloat16
f32 = jnp.float32
VOCAB_AXES = ("x", "z", "core")
SIDE = 4


def shift_pairs(step):
    return [(place, (place + step) % SIDE) for place in range(SIDE)]


def dot(left, right):
    return jnp.dot(left, right, preferred_element_type=f32)


def swap_core(value):
    return lax.ppermute(value, "core", [(0, 1), (1, 0)])


def transpose_plane(value):
    pairs = [(a * SIDE + b, b * SIDE + a) for a in range(SIDE) for b in range(SIDE)]
    return lax.ppermute(value, ("group", "x"), pairs)


def piece_at(value, place, dimension):
    size = value.shape[dimension] // SIDE
    return lax.dynamic_slice_in_dim(value, place * size, size, dimension)


def scatter_sum(value, axis, dimension):
    place = lax.axis_index(axis)
    total = piece_at(value, place, dimension).astype(f32)
    for step in (1, 3, 2):
        sent = piece_at(value, (place + step) % SIDE, dimension).astype(bf16)
        total = total + lax.ppermute(sent, axis, shift_pairs(step)).astype(f32)
    return total


def exchange(value, axis, dimension):
    place = lax.axis_index(axis)
    moved = [piece_at(value, place, dimension)]
    for step in (1, 2, 3):
        sent = piece_at(value, (place + step) % SIDE, dimension)
        moved.append(lax.ppermute(sent, axis, shift_pairs(step)))
    return moved


def in_order(moved, axis, dimension):
    place = lax.axis_index(axis)
    size = moved[0].shape[dimension]
    ordered = [moved[3], moved[2], moved[1], moved[0], moved[3], moved[2], moved[1]]
    stacked = jnp.concatenate(ordered, axis=dimension)
    return lax.dynamic_slice_in_dim(stacked, (3 - place) * size, SIDE * size, dimension)


def gather_along(value, axis, dimension):
    moved = [value] + [lax.ppermute(value, axis, shift_pairs(step)) for step in (1, 2, 3)]
    return in_order(moved, axis, dimension)


def gather_small(value):
    copies = jnp.broadcast_to(value[None], (32,) + value.shape)
    return lax.all_to_all(copies, VOCAB_AXES, split_axis=0, concat_axis=0, tiled=True)


def peak_and_sum(scores):
    peak = jnp.max(scores, axis=1)
    return peak, jnp.sum(jnp.exp(scores - peak[:, None]), axis=1)


def log_sums(peaks, totals):
    top = jnp.max(peaks, axis=0)
    return top + jnp.log(jnp.sum(totals * jnp.exp(peaks - top[None]), axis=0))


def crossed_pairs(step, turn):
    pairs = []
    for x in range(SIDE):
        for z in range(SIDE):
            for core in range(2):
                to_x, to_z = (x + step) % SIDE, (z + step) % SIDE
                target = (to_x, z) if core == turn else (x, to_z)
                pairs.append(((x * SIDE + z) * 2 + core, (target[0] * SIDE + target[1]) * 2 + core))
    return pairs


def crossed(value, step, turn):
    return lax.ppermute(value, VOCAB_AXES, crossed_pairs(step, turn))


def by_core(mine, core):
    theirs = swap_core(mine)
    return jnp.where(core == 0, mine, theirs), jnp.where(core == 0, theirs, mine)


def assemble_kernel(first_hop, places, gain, *refs):
    mine, theirs = refs[:SIDE], refs[SIDE : 2 * SIDE]
    out, squares, held = refs[2 * SIDE :]
    group, core = places[0], places[3]
    block_rows = held.shape[0]
    slab = block_rows // 2

    def one(index, _):
        number, quarter = index // SIDE, lax.rem(index, SIDE)
        hop = number + first_hop
        ahead = jnp.where(hop == 0, 2, jnp.where(hop == 3, 0, jnp.where(hop == 1, 1, -1)))
        block = lax.rem(group + jnp.where(quarter < 2, -ahead, ahead) + SIDE, SIDE)
        owner = block // 2
        lower = lax.rem(block, 2) == 0
        place = jnp.where(owner == 0, places[1], places[2])
        source = lax.rem(place - quarter + SIDE, SIDE)
        for step in range(SIDE):
            for own, pieces in ((True, mine), (False, theirs)):

                @pl.when((source == step) & ((owner == core) == own))
                def _(ref=pieces[step]):
                    held[...] = ref[...]

        for part in range(slab // 16):
            values = held[part * 32 : (part + 1) * 32, :].astype(f32)
            even = jnp.concatenate([values[0:8], values[16:24]])
            odd = jnp.concatenate([values[8:16], values[24:32]])
            chosen = jnp.where(lower, even, odd)
            rows = pl.ds(pl.multiple_of(quarter * slab + part * 16, 16), 16)
            squares[number, rows, :] = jnp.sum(chosen * chosen, axis=1, keepdims=True)
            out[number, rows, :] = (chosen * gain[...]).astype(bf16)
        return 0

    lax.fori_loop(0, out.shape[0] * SIDE, one, 0)


def assemble(first_hop, count, places, gain, mine, theirs, rows):
    width = gain.shape[0]
    vmem = pl.BlockSpec(memory_space=pltpu.VMEM)
    return pl.pallas_call(
        functools.partial(assemble_kernel, first_hop),
        out_shape=(
            jax.ShapeDtypeStruct((count, rows, width), bf16),
            jax.ShapeDtypeStruct((count, rows, 1), f32),
        ),
        in_specs=[pl.BlockSpec(memory_space=pltpu.SMEM)] + [vmem] * (1 + 2 * SIDE),
        out_specs=(vmem, vmem),
        scratch_shapes=[pltpu.VMEM((rows // 2, width), bf16)],
        compiler_params=pltpu.CompilerParams(vmem_limit_bytes=8 * 1024 * 1024),
        cost_estimate=pl.CostEstimate(
            flops=count * rows * width * 4, bytes_accessed=count * rows * width * 4, transcendentals=0
        ),
    )(places, gain.reshape(1, width), *mine, *theirs)


def embed_kernel(full_width, places, gain, *refs):
    pieces, out = refs[:SIDE], refs[SIDE]
    values = [piece[...].astype(f32) for piece in pieces]
    total = sum(jnp.sum(value * value, axis=1, keepdims=True) for value in values)
    scale = lax.rsqrt(total / full_width + epsilon)
    pair_rows, pair_width = out.shape[1:]
    for step in range(SIDE):
        place = lax.rem(places[0] - step + SIDE, SIDE)
        normed = (values[step] * scale * gain[place]).astype(bf16)
        for z in range(SIDE):
            for core in range(2):
                out[place * 2 * SIDE + z * 2 + core] = normed[
                    core * pair_rows : (core + 1) * pair_rows, z * pair_width : (z + 1) * pair_width
                ]


def embed_slices(places, gain, pieces, full_width, shards):
    look, quarter = pieces[0].shape
    vmem = pl.BlockSpec(memory_space=pltpu.VMEM)
    return pl.pallas_call(
        functools.partial(embed_kernel, full_width),
        out_shape=jax.ShapeDtypeStruct((shards, look // 2, quarter // SIDE), bf16),
        in_specs=[pl.BlockSpec(memory_space=pltpu.SMEM)] + [vmem] * (1 + SIDE),
        out_specs=vmem,
        compiler_params=pltpu.CompilerParams(vmem_limit_bytes=6 * 1024 * 1024),
        cost_estimate=pl.CostEstimate(
            flops=look * full_width * 4, bytes_accessed=look * full_width * 4, transcendentals=0
        ),
    )(places, gain.reshape(SIDE, 1, quarter), *pieces)


def state_kernel(places, hidden_pair, hidden_weight, embed_pair, embed_weight, own, *refs):
    sent, held = refs[:3], refs[3]
    rows, width = own.shape
    outer = jnp.where(places[3] == 0, places[1], places[2])
    lanes = held.shape[1]
    for part in range(width // lanes):
        columns = slice(part * lanes, (part + 1) * lanes)
        terms = dot(hidden_pair[...], hidden_weight[:, columns])
        held[...] = terms + dot(embed_pair[...], embed_weight[:, columns])
        for step, out in ((2, sent[0]), (1, sent[1]), (3, sent[2]), (0, own)):
            place = lax.rem(outer + step, SIDE)
            cut = pl.ds(pl.multiple_of(place * rows, rows), rows)
            out[:, columns] = held[cut, :].astype(out.dtype)


def state_blocks(places, hidden_pair, hidden_weight, embed_pair, embed_weight):
    rows, depth = hidden_pair.shape
    width = hidden_weight.shape[1]
    vmem = pl.BlockSpec(memory_space=pltpu.VMEM)
    block = (rows // SIDE, width)
    return pl.pallas_call(
        state_kernel,
        out_shape=(jax.ShapeDtypeStruct(block, f32),) + (jax.ShapeDtypeStruct(block, bf16),) * 3,
        in_specs=[pl.BlockSpec(memory_space=pltpu.SMEM)] + [vmem] * 4,
        out_specs=(vmem,) * 4,
        scratch_shapes=[pltpu.VMEM((rows, width // 7), f32)],
        compiler_params=pltpu.CompilerParams(vmem_limit_bytes=10 * 1024 * 1024),
        cost_estimate=pl.CostEstimate(
            flops=rows * width * depth * 4, bytes_accessed=depth * width * 8, transcendentals=0
        ),
    )(places, hidden_pair, hidden_weight, embed_pair, embed_weight)


def per_device(
    hidden,
    main_gain,
    head_weight,
    token_owner,
    token_offset,
    embed_table,
    hidden_gain,
    embed_gain,
    hidden_projection,
    embed_projection,
    draft_gain,
):
    group = lax.axis_index("group")
    x_place = lax.axis_index("x")
    z_place = lax.axis_index("z")
    core = lax.axis_index("core")
    vocab = (x_place * SIDE + z_place) * 2 + core
    rows, slice_width = hidden.shape
    full_width = main_gain.shape[0]
    quarter = full_width // SIDE

    hidden_values = hidden.astype(f32)

    places = jnp.stack([group, x_place, z_place, core]).astype(jnp.int32)

    main_slice = lax.dynamic_slice_in_dim(main_gain, vocab * slice_width, slice_width, 0)
    main_piece = (hidden_values * main_slice).astype(bf16).T

    shards = 32
    capacity = 4
    owner_block = token_owner.astype(f32)
    token_block = (owner_block * 2048.0 + token_offset.astype(f32)).reshape(-1)
    look = token_block.shape[0]
    squares = jnp.sum(hidden_values * hidden_values, axis=1)
    own_block, main_piece = lax.optimization_barrier(
        (jnp.concatenate([token_block, squares]), main_piece)
    )
    gathered = gather_small(own_block)
    main_moved = transpose_plane(main_piece)
    hidden_scale = lax.rsqrt(jnp.sum(gathered[:, look:], axis=0) / full_width + epsilon)

    tokens = gathered[:, :look].astype(jnp.int32)
    wanted = (tokens // 2048) == vocab
    rank = jnp.cumsum(wanted.astype(jnp.int32), axis=1) - 1
    slot = jnp.arange(capacity, dtype=jnp.int32)
    chosen = wanted[:, None, :] & (rank[:, None, :] == slot[None, :, None])
    requests = jnp.sum(jnp.where(chosen, (tokens % 2048)[:, None, :], 0), axis=2).reshape(-1)
    table_rows = embed_table.shape[0]
    pick = (requests[:, None] == jnp.arange(table_rows, dtype=jnp.int32)[None, :]).astype(bf16)
    found = dot(pick, embed_table).astype(bf16)
    hidden_slice = lax.dynamic_slice_in_dim(hidden_gain, vocab * slice_width, slice_width, 0)
    hidden_piece = (hidden_values * hidden_scale[:, None] * hidden_slice).astype(bf16)
    block_rows = rows // shards
    pair_rows = 2 * block_rows
    pair_width = 2 * slice_width

    found, group_later, hidden_piece, main_moved = lax.optimization_barrier(
        (found, group, hidden_piece, main_moved)
    )
    main_stack = lax.all_gather(main_moved, VOCAB_AXES, axis=0, tiled=True).reshape(
        SIDE, quarter, rows
    )

    def both_slices(weight):
        mine = lax.dynamic_slice_in_dim(weight, group_later * quarter, quarter, 1)
        return jnp.concatenate(by_core(mine, core))

    hidden_weight = both_slices(hidden_projection)
    embed_weight = both_slices(embed_projection)

    hidden_moved = [hidden_piece]
    hidden_moved += [lax.ppermute(hidden_piece, "group", shift_pairs(step)) for step in (1, 2, 3)]

    hidden_all = jnp.stack(hidden_moved)

    def pair_of(stacked, which):
        taken = [
            lax.dynamic_index_in_dim(stacked, (group - 2 * which - e) % SIDE, 0, keepdims=False)
            for e in range(2)
        ]
        return jnp.stack(taken)

    own = pair_of(hidden_all, core)
    other = swap_core(pair_of(hidden_all, 1 - core))
    hidden_pair = jnp.concatenate(
        [jnp.where(core == 0, own, other), jnp.where(core == 0, other, own)], axis=2
    ).reshape(2, shards, block_rows, pair_width)
    hidden_pair = hidden_pair.transpose(1, 0, 2, 3).reshape(shards * pair_rows, pair_width)
    returned = lax.all_to_all(
        found.reshape(shards, capacity, quarter), VOCAB_AXES, split_axis=0, concat_axis=0, tiled=True
    ).reshape(shards * capacity, quarter)
    owners = lax.dynamic_index_in_dim(tokens, vocab, 0, keepdims=False) // 2048
    matches = owners[:, None] == jnp.arange(shards, dtype=jnp.int32)[None, :]
    earlier = jnp.cumsum(matches.astype(jnp.int32), axis=0) - 1
    own_rank = jnp.sum(jnp.where(matches, earlier, 0), axis=1)
    place = owners * capacity + own_rank
    put = (place[:, None] == jnp.arange(shards * capacity, dtype=jnp.int32)[None, :]).astype(bf16)
    fetched = dot(put, returned).astype(bf16)
    fetched_moved = [fetched]
    fetched_moved += [lax.ppermute(fetched, "group", shift_pairs(step)) for step in (1, 2, 3)]
    fetched_moved, hidden_weight, embed_weight, hidden_pair = lax.optimization_barrier(
        (fetched_moved, hidden_weight, embed_weight, hidden_pair)
    )
    send = embed_slices(places, embed_gain, fetched_moved, full_width, shards)
    embed_pair = lax.all_to_all(
        send, VOCAB_AXES, split_axis=0, concat_axis=0, tiled=True
    ).reshape(shards * pair_rows, pair_width)

    state_gain = lax.dynamic_slice_in_dim(draft_gain, group * quarter, quarter, 0)

    total, *sent = state_blocks(
        places, hidden_pair, hidden_weight, embed_pair, embed_weight
    )
    moved = [crossed(block, step, 0) for block, step in zip(sent, (2, 1, 3))]
    main_partial = jnp.einsum(
        "gkr,kn->grn", main_stack, head_weight, preferred_element_type=f32
    ).astype(bf16)
    moved, main_partial = lax.optimization_barrier((moved, main_partial))
    main_raw = lax.psum_scatter(
        main_partial.reshape(SIDE * rows, -1), "group", scatter_dimension=0, tiled=True
    )
    for piece in moved:
        total = total + piece.astype(f32)
    sent = total.astype(bf16)
    for step in (2, 1, 3):
        total = total + crossed(sent, step, 1).astype(f32)
    sent = total.astype(bf16)
    mine = [sent] + [crossed(sent, step, 0) for step in (1, 2, 3)]
    theirs = [swap_core(piece) for piece in mine]
    put_together = functools.partial(
        assemble, places=places, gain=state_gain, mine=mine, theirs=theirs, rows=rows
    )
    half = rows // 2
    (far, near), (far_squares, near_squares) = put_together(0, 2)
    far_terms = dot(far, head_weight).astype(bf16)
    far_up = lax.ppermute(far_terms[:half], "group", shift_pairs(1))
    far_down = lax.ppermute(far_terms[half:], "group", shift_pairs(3))
    near_terms = dot(near, head_weight).astype(bf16)
    near_up = lax.ppermute(near_terms[half:], "group", shift_pairs(1))
    near_down = lax.ppermute(near_terms[:half], "group", shift_pairs(3))
    near_terms, places_later = lax.optimization_barrier((near_terms, places))
    (passing, own), (passing_squares, own_squares) = put_together(2, 2, places=places_later)
    passing_terms = dot(passing, head_weight)
    passing_up = (passing_terms[:half] + far_up.astype(f32)).astype(bf16)
    passing_down = (passing_terms[half:] + far_down.astype(f32)).astype(bf16)
    passed_up = lax.ppermute(passing_up, "group", shift_pairs(1))
    passed_down = lax.ppermute(passing_down, "group", shift_pairs(3))
    own_terms = dot(own, head_weight)
    near_up, near_down, main_raw, far_squares, near_squares, passing_squares, _, _ = (
        lax.optimization_barrier(
            (
                near_up,
                near_down,
                main_raw,
                far_squares,
                near_squares,
                passing_squares,
                passing_up,
                passing_down,
            )
        )
    )
    near_squares, passing_squares = near_squares[:, 0], passing_squares[:, 0]
    state_squares = own_squares[:, 0]
    for step, sent in (
        (1, jnp.concatenate([passing_squares[:half], near_squares[half:]])),
        (3, jnp.concatenate([near_squares[:half], passing_squares[half:]])),
        (2, far_squares[:, 0]),
    ):
        state_squares = state_squares + lax.ppermute(sent, "group", shift_pairs(step))
    draft_scale = lax.rsqrt(state_squares / full_width + epsilon)
    main_scores = main_raw.astype(f32) * hidden_scale[:, None]
    main_stats = peak_and_sum(main_scores)
    upper = own_terms[:half] + near_down.astype(f32)
    lower = own_terms[half:] + near_up.astype(f32)
    upper, lower, main_stats, draft_scale, passed_up, passed_down = lax.optimization_barrier(
        (upper, lower, main_stats, draft_scale, passed_up, passed_down)
    )
    draft_scores = jnp.concatenate([upper + passed_up.astype(f32), lower + passed_down.astype(f32)])
    draft_scores = draft_scores * draft_scale[:, None]
    stats = jnp.concatenate(main_stats + peak_and_sum(draft_scores))
    every = gather_small(stats).reshape(shards, 4, rows)
    main_out = (main_scores - log_sums(every[:, 0], every[:, 1])[:, None]).astype(bf16)
    draft_out = (draft_scores - log_sums(every[:, 2], every[:, 3])[:, None]).astype(bf16)
    return main_out, draft_out


def solution(mesh):
    vocab = mesh.shape["vocab"]
    whole = Mesh(
        mesh.devices.reshape(SIDE, SIDE, vocab // SIDE // 2, 2), ("group", "x", "z", "core")
    )
    placed = (
        P("group", VOCAB_AXES),
        P(),
        P("group", VOCAB_AXES),
        P(VOCAB_AXES, None, None, None),
        P(VOCAB_AXES, None, None, None),
        P(VOCAB_AXES, "group"),
        P(),
        P(),
        P(VOCAB_AXES, None),
        P(VOCAB_AXES, None),
        P(),
    )
    return jax.shard_map(
        per_device,
        mesh=whole,
        in_specs=placed,
        out_specs=(P("group", VOCAB_AXES), P("group", VOCAB_AXES)),
        check_vma=False,
    )
```

```python
import functools

import jax
import jax.numpy as jnp
from jax import lax
from jax.experimental import pallas as pl
from jax.experimental.pallas import tpu as pltpu
from jax.sharding import Mesh, PartitionSpec as P

epsilon = 1e-06
bf16 = jnp.bfloat16
f32 = jnp.float32
VOCAB_AXES = ("x", "z", "core")
SIDE = 4


def shift_pairs(step):
    return [(place, (place + step) % SIDE) for place in range(SIDE)]


def dot(left, right):
    return jnp.dot(left, right, preferred_element_type=f32)


def swap_core(value):
    return lax.ppermute(value, "core", [(0, 1), (1, 0)])


def transpose_plane(value):
    pairs = [(a * SIDE + b, b * SIDE + a) for a in range(SIDE) for b in range(SIDE)]
    return lax.ppermute(value, ("group", "x"), pairs)


def piece_at(value, place, dimension):
    size = value.shape[dimension] // SIDE
    return lax.dynamic_slice_in_dim(value, place * size, size, dimension)


def scatter_sum(value, axis, dimension):
    place = lax.axis_index(axis)
    total = piece_at(value, place, dimension).astype(f32)
    for step in (1, 3, 2):
        sent = piece_at(value, (place + step) % SIDE, dimension).astype(bf16)
        total = total + lax.ppermute(sent, axis, shift_pairs(step)).astype(f32)
    return total


def exchange(value, axis, dimension):
    place = lax.axis_index(axis)
    moved = [piece_at(value, place, dimension)]
    for step in (1, 2, 3):
        sent = piece_at(value, (place + step) % SIDE, dimension)
        moved.append(lax.ppermute(sent, axis, shift_pairs(step)))
    return moved


def in_order(moved, axis, dimension):
    place = lax.axis_index(axis)
    size = moved[0].shape[dimension]
    ordered = [moved[3], moved[2], moved[1], moved[0], moved[3], moved[2], moved[1]]
    stacked = jnp.concatenate(ordered, axis=dimension)
    return lax.dynamic_slice_in_dim(stacked, (3 - place) * size, SIDE * size, dimension)


def gather_along(value, axis, dimension):
    moved = [value] + [lax.ppermute(value, axis, shift_pairs(step)) for step in (1, 2, 3)]
    return in_order(moved, axis, dimension)


def gather_small(value):
    copies = jnp.broadcast_to(value[None], (32,) + value.shape)
    return lax.all_to_all(copies, VOCAB_AXES, split_axis=0, concat_axis=0, tiled=True)


def peak_and_sum(scores):
    peak = jnp.max(scores, axis=1)
    return peak, jnp.sum(jnp.exp(scores - peak[:, None]), axis=1)


def log_sums(peaks, totals):
    top = jnp.max(peaks, axis=0)
    return top + jnp.log(jnp.sum(totals * jnp.exp(peaks - top[None]), axis=0))


def crossed_pairs(step, turn):
    pairs = []
    for x in range(SIDE):
        for z in range(SIDE):
            for core in range(2):
                to_x, to_z = (x + step) % SIDE, (z + step) % SIDE
                target = (to_x, z) if core == turn else (x, to_z)
                pairs.append(((x * SIDE + z) * 2 + core, (target[0] * SIDE + target[1]) * 2 + core))
    return pairs


def crossed(value, step, turn):
    return lax.ppermute(value, VOCAB_AXES, crossed_pairs(step, turn))


def by_core(mine, core):
    theirs = swap_core(mine)
    return jnp.where(core == 0, mine, theirs), jnp.where(core == 0, theirs, mine)


def head_kernel(ahead, places, gain, weight, *refs):
    upper_out, lower_out, squares, held, inputs = refs[-5:]
    blocks = refs[:-5]
    parts = len(blocks) // (2 * SIDE)
    group, core = places[0], places[3]
    slab = held.shape[0]
    far = lax.rem(group + 2, SIDE)
    beside = group + 1 - 2 * lax.rem(group, 2)

    def one(quarter, _):
        block = lax.rem(group + jnp.where(quarter < 2, -ahead, ahead) + SIDE, SIDE)
        owner = block // 2
        early = (block == far) | (block == beside)
        place = jnp.where(owner == 0, places[1], places[2])
        source = lax.rem(place - quarter + SIDE, SIDE)
        for part in range(parts):
            for own in range(2):
                for step in range(SIDE):
                    ref = blocks[(part * 2 + own) * SIDE + step]

                    @pl.when((source == step) & ((owner == core) == (own == 0)) & (early == (part == 0)))
                    def _(ref=ref):
                        held[...] = ref[...]

        for part in range(slab // 16):
            values = held[part * 16 : (part + 1) * 16, :].astype(f32)
            rows = pl.ds(pl.multiple_of(quarter * slab + part * 16, 16), 16)
            squares[rows, :] = jnp.sum(values * values, axis=1, keepdims=True)
            inputs[rows, :] = (values * gain[...]).astype(bf16)
        return 0

    lax.fori_loop(0, SIDE, one, 0)
    half = upper_out.shape[0]
    width = weight.shape[1]
    lanes = width // SIDE
    for part in range(SIDE):
        columns = slice(part * lanes, (part + 1) * lanes)
        terms = dot(inputs[...], weight[:, columns]).astype(bf16)
        upper_out[:, columns] = terms[:half]
        lower_out[:, columns] = terms[half:]
    upper_out[:, width:] = two_parts(squares[:half, :])
    lower_out[:, width:] = two_parts(squares[half:, :])


def head_set(ahead, places, blocks, gain, weight, rows):
    depth, width = weight.shape
    vmem = pl.BlockSpec(memory_space=pltpu.VMEM)
    return pl.pallas_call(
        functools.partial(head_kernel, ahead),
        out_shape=(jax.ShapeDtypeStruct((rows // 2, width + 128), bf16),) * 2,
        in_specs=[pl.BlockSpec(memory_space=pltpu.SMEM)] + [vmem] * (2 + len(blocks)),
        out_specs=(vmem,) * 2,
        scratch_shapes=[
            pltpu.VMEM((rows, 1), f32),
            pltpu.VMEM((rows // SIDE, depth), bf16),
            pltpu.VMEM((rows, depth), bf16),
        ],
        compiler_params=pltpu.CompilerParams(vmem_limit_bytes=24 * 1024 * 1024),
        cost_estimate=pl.CostEstimate(
            flops=rows * depth * width * 2, bytes_accessed=0, transcendentals=0
        ),
    )(places, gain.reshape(1, depth), weight, *blocks)


def two_parts(total):
    shape = (total.shape[0], 128)
    column = lax.broadcasted_iota(jnp.int32, shape, 1)
    high = total.astype(bf16).astype(f32)
    rest = jnp.where(column == 1, jnp.broadcast_to(total - high, shape), 0.0)
    return jnp.where(column == 0, jnp.broadcast_to(high, shape), rest).astype(bf16)


def add_kernel(first, first_more, second, second_more, first_out, second_out):
    width = first.shape[1] - 128
    for one, more, out in ((first, first_more, first_out), (second, second_more, second_out)):
        total = one[:, :width].astype(f32) + more[:, :width].astype(f32)
        out[:, :width] = total.astype(bf16)
        squares = one[:, width:].astype(f32) + more[:, width:].astype(f32)
        out[:, width:] = two_parts(jnp.sum(squares, axis=1, keepdims=True))


def add_both(first, first_more, second, second_more):
    vmem = pl.BlockSpec(memory_space=pltpu.VMEM)
    return pl.pallas_call(
        add_kernel,
        out_shape=(jax.ShapeDtypeStruct(first.shape, bf16),) * 2,
        in_specs=[vmem] * 4,
        out_specs=(vmem,) * 2,
        compiler_params=pltpu.CompilerParams(vmem_limit_bytes=8 * 1024 * 1024),
        cost_estimate=pl.CostEstimate(flops=first.size * 2, bytes_accessed=0, transcendentals=0),
    )(first, first_more, second, second_more)


def embed_kernel(full_width, places, gain, *refs):
    pieces, out = refs[:SIDE], refs[SIDE]
    values = [piece[...].astype(f32) for piece in pieces]
    total = sum(jnp.sum(value * value, axis=1, keepdims=True) for value in values)
    scale = lax.rsqrt(total / full_width + epsilon)
    pair_rows, pair_width = out.shape[1:]
    for step in range(SIDE):
        place = lax.rem(places[0] - step + SIDE, SIDE)
        normed = (values[step] * scale * gain[place]).astype(bf16)
        for z in range(SIDE):
            for core in range(2):
                out[place * 2 * SIDE + z * 2 + core] = normed[
                    core * pair_rows : (core + 1) * pair_rows, z * pair_width : (z + 1) * pair_width
                ]


def embed_slices(places, gain, pieces, full_width, shards):
    look, quarter = pieces[0].shape
    vmem = pl.BlockSpec(memory_space=pltpu.VMEM)
    return pl.pallas_call(
        functools.partial(embed_kernel, full_width),
        out_shape=jax.ShapeDtypeStruct((shards, look // 2, quarter // SIDE), bf16),
        in_specs=[pl.BlockSpec(memory_space=pltpu.SMEM)] + [vmem] * (1 + SIDE),
        out_specs=vmem,
        compiler_params=pltpu.CompilerParams(vmem_limit_bytes=6 * 1024 * 1024),
        cost_estimate=pl.CostEstimate(
            flops=look * full_width * 4, bytes_accessed=look * full_width * 4, transcendentals=0
        ),
    )(places, gain.reshape(SIDE, 1, quarter), *pieces)


def state_kernel(places, hidden_pair, hidden_weight, embed_pair, embed_weight, own, *refs):
    sent, held = refs[:3], refs[3]
    rows, width = own.shape
    outer = jnp.where(places[3] == 0, places[1], places[2])
    lanes = held.shape[1]
    for part in range(width // lanes):
        columns = slice(part * lanes, (part + 1) * lanes)
        terms = dot(hidden_pair[...], hidden_weight[:, columns])
        held[...] = terms + dot(embed_pair[...], embed_weight[:, columns])
        for step, out in ((2, sent[0]), (1, sent[1]), (3, sent[2]), (0, own)):
            place = lax.rem(outer + step, SIDE)
            cut = pl.ds(pl.multiple_of(place * rows, rows), rows)
            out[:, columns] = held[cut, :].astype(out.dtype)


def state_blocks(places, hidden_pair, hidden_weight, embed_pair, embed_weight):
    rows, depth = hidden_pair.shape
    width = hidden_weight.shape[1]
    vmem = pl.BlockSpec(memory_space=pltpu.VMEM)
    block = (rows // SIDE, width)
    return pl.pallas_call(
        state_kernel,
        out_shape=(jax.ShapeDtypeStruct(block, f32),) + (jax.ShapeDtypeStruct(block, bf16),) * 3,
        in_specs=[pl.BlockSpec(memory_space=pltpu.SMEM)] + [vmem] * 4,
        out_specs=(vmem,) * 4,
        scratch_shapes=[pltpu.VMEM((rows, width // 7), f32)],
        compiler_params=pltpu.CompilerParams(vmem_limit_bytes=10 * 1024 * 1024),
        cost_estimate=pl.CostEstimate(
            flops=rows * width * depth * 4, bytes_accessed=depth * width * 8, transcendentals=0
        ),
    )(places, hidden_pair, hidden_weight, embed_pair, embed_weight)


def per_device(
    hidden,
    main_gain,
    head_weight,
    token_owner,
    token_offset,
    embed_table,
    hidden_gain,
    embed_gain,
    hidden_projection,
    embed_projection,
    draft_gain,
):
    group = lax.axis_index("group")
    x_place = lax.axis_index("x")
    z_place = lax.axis_index("z")
    core = lax.axis_index("core")
    vocab = (x_place * SIDE + z_place) * 2 + core
    rows, slice_width = hidden.shape
    full_width = main_gain.shape[0]
    quarter = full_width // SIDE

    hidden_values = hidden.astype(f32)

    places = jnp.stack([group, x_place, z_place, core]).astype(jnp.int32)

    main_slice = lax.dynamic_slice_in_dim(main_gain, vocab * slice_width, slice_width, 0)
    main_piece = (hidden_values * main_slice).astype(bf16).T

    shards = 32
    capacity = 4
    owner_block = token_owner.astype(f32)
    token_block = (owner_block * 2048.0 + token_offset.astype(f32)).reshape(-1)
    look = token_block.shape[0]
    squares = jnp.sum(hidden_values * hidden_values, axis=1)
    own_block, main_piece = lax.optimization_barrier(
        (jnp.concatenate([token_block, squares]), main_piece)
    )
    gathered = gather_small(own_block)
    main_moved = transpose_plane(main_piece)
    hidden_scale = lax.rsqrt(jnp.sum(gathered[:, look:], axis=0) / full_width + epsilon)

    tokens = gathered[:, :look].astype(jnp.int32)
    wanted = (tokens // 2048) == vocab
    rank = jnp.cumsum(wanted.astype(jnp.int32), axis=1) - 1
    slot = jnp.arange(capacity, dtype=jnp.int32)
    chosen = wanted[:, None, :] & (rank[:, None, :] == slot[None, :, None])
    requests = jnp.sum(jnp.where(chosen, (tokens % 2048)[:, None, :], 0), axis=2).reshape(-1)
    table_rows = embed_table.shape[0]
    pick = (requests[:, None] == jnp.arange(table_rows, dtype=jnp.int32)[None, :]).astype(bf16)
    found = dot(pick, embed_table).astype(bf16)
    hidden_slice = lax.dynamic_slice_in_dim(hidden_gain, vocab * slice_width, slice_width, 0)
    hidden_piece = (hidden_values * hidden_scale[:, None] * hidden_slice).astype(bf16)
    block_rows = rows // shards
    pair_rows = 2 * block_rows
    pair_width = 2 * slice_width

    found, group_later, hidden_piece, main_moved = lax.optimization_barrier(
        (found, group, hidden_piece, main_moved)
    )
    main_stack = lax.all_gather(main_moved, VOCAB_AXES, axis=0, tiled=True).reshape(
        SIDE, quarter, rows
    )

    def both_slices(weight):
        mine = lax.dynamic_slice_in_dim(weight, group_later * quarter, quarter, 1)
        return jnp.concatenate(by_core(mine, core))

    hidden_weight = both_slices(hidden_projection)
    embed_weight = both_slices(embed_projection)

    hidden_moved = [hidden_piece]
    hidden_moved += [lax.ppermute(hidden_piece, "group", shift_pairs(step)) for step in (1, 2, 3)]

    hidden_all = jnp.stack(hidden_moved)

    def pair_of(stacked, which):
        taken = [
            lax.dynamic_index_in_dim(stacked, (group - 2 * which - e) % SIDE, 0, keepdims=False)
            for e in range(2)
        ]
        return jnp.stack(taken)

    own = pair_of(hidden_all, core)
    other = swap_core(pair_of(hidden_all, 1 - core))
    hidden_pair = jnp.concatenate(
        [jnp.where(core == 0, own, other), jnp.where(core == 0, other, own)], axis=2
    ).reshape(2, shards, block_rows, pair_width)
    hidden_pair = hidden_pair.transpose(1, 0, 2, 3).reshape(shards * pair_rows, pair_width)
    returned = lax.all_to_all(
        found.reshape(shards, capacity, quarter), VOCAB_AXES, split_axis=0, concat_axis=0, tiled=True
    ).reshape(shards * capacity, quarter)
    owners = lax.dynamic_index_in_dim(tokens, vocab, 0, keepdims=False) // 2048
    matches = owners[:, None] == jnp.arange(shards, dtype=jnp.int32)[None, :]
    earlier = jnp.cumsum(matches.astype(jnp.int32), axis=0) - 1
    own_rank = jnp.sum(jnp.where(matches, earlier, 0), axis=1)
    place = owners * capacity + own_rank
    put = (place[:, None] == jnp.arange(shards * capacity, dtype=jnp.int32)[None, :]).astype(bf16)
    fetched = dot(put, returned).astype(bf16)
    fetched_moved = [fetched]
    fetched_moved += [lax.ppermute(fetched, "group", shift_pairs(step)) for step in (1, 2, 3)]
    fetched_moved, hidden_weight, embed_weight, hidden_pair = lax.optimization_barrier(
        (fetched_moved, hidden_weight, embed_weight, hidden_pair)
    )
    send = embed_slices(places, embed_gain, fetched_moved, full_width, shards)
    embed_pair = lax.all_to_all(
        send, VOCAB_AXES, split_axis=0, concat_axis=0, tiled=True
    ).reshape(shards * pair_rows, pair_width)

    state_gain = lax.dynamic_slice_in_dim(draft_gain, group * quarter, quarter, 0)

    total, *sent = state_blocks(
        places, hidden_pair, hidden_weight, embed_pair, embed_weight
    )
    moved = [crossed(block, step, 0) for block, step in zip(sent, (2, 1, 3))]
    main_partial = jnp.einsum(
        "gkr,kn->grn", main_stack, head_weight, preferred_element_type=f32
    ).astype(bf16)
    moved, main_partial = lax.optimization_barrier((moved, main_partial))
    main_raw = lax.psum_scatter(
        main_partial.reshape(SIDE * rows, -1), "group", scatter_dimension=0, tiled=True
    )
    for piece in moved:
        total = total + piece.astype(f32)
    sent = total.astype(bf16)
    for step in (2, 1, 3):
        total = total + crossed(sent, step, 1).astype(f32)
    far_core = (group + 2) % SIDE // 2
    early = jnp.where(core == far_core, group % 2, 1 - group % 2)
    by_group = total.reshape(shards // SIDE, 2, block_rows, quarter)
    sent, later = [
        lax.dynamic_index_in_dim(by_group, which, 1, keepdims=False)
        .astype(bf16)
        .reshape(rows // SIDE, quarter)
        for which in (early, 1 - early)
    ]
    early_mine = [sent] + [crossed(sent, step, 0) for step in (1, 2, 3)]
    early_mine, later = lax.optimization_barrier((early_mine, later))
    late_mine = [later] + [crossed(later, step, 0) for step in (1, 2, 3)]
    blocks = early_mine + [swap_core(piece) for piece in early_mine]
    half = rows // 2

    head = functools.partial(head_set, gain=state_gain, weight=head_weight, rows=rows)
    far_upper, far_lower = head(2, places, blocks)
    far_upper, far_lower, late_mine = lax.optimization_barrier((far_upper, far_lower, late_mine))
    far_up = lax.ppermute(far_upper, "group", shift_pairs(1))
    far_down = lax.ppermute(far_lower, "group", shift_pairs(3))
    blocks = blocks + late_mine + [swap_core(piece) for piece in late_mine]
    near_upper, near_lower = head(1, places, blocks)
    near_up = lax.ppermute(near_lower, "group", shift_pairs(1))
    near_down = lax.ppermute(near_upper, "group", shift_pairs(3))
    near_upper, places_later = lax.optimization_barrier((near_upper, places))
    passing_upper, passing_lower = head(-1, places_later, blocks)
    passing_upper, passing_lower = add_both(passing_upper, far_up, passing_lower, far_down)
    passed_up = lax.ppermute(passing_upper, "group", shift_pairs(1))
    passed_down = lax.ppermute(passing_lower, "group", shift_pairs(3))
    passing_upper, places_later = lax.optimization_barrier((passing_upper, places))
    own_upper, own_lower = head(0, places_later, blocks)
    main_scores = main_raw.astype(f32) * hidden_scale[:, None]
    main_stats = peak_and_sum(main_scores)
    near_up, near_down, own_upper, own_lower, main_stats = lax.optimization_barrier(
        (near_up, near_down, own_upper, own_lower, main_stats)
    )
    upper = own_upper.astype(f32) + near_down.astype(f32)
    lower = own_lower.astype(f32) + near_up.astype(f32)
    draft_raw = jnp.concatenate([upper + passed_up.astype(f32), lower + passed_down.astype(f32)])
    head_width = head_weight.shape[1]
    state_squares = jnp.sum(draft_raw[:, head_width:], axis=1)
    draft_scale = lax.rsqrt(state_squares / full_width + epsilon)
    draft_scores = draft_raw[:, :head_width] * draft_scale[:, None]
    stats = jnp.concatenate(main_stats + peak_and_sum(draft_scores))
    every = gather_small(stats).reshape(shards, 4, rows)
    main_out = (main_scores - log_sums(every[:, 0], every[:, 1])[:, None]).astype(bf16)
    draft_out = (draft_scores - log_sums(every[:, 2], every[:, 3])[:, None]).astype(bf16)
    return main_out, draft_out


def solution(mesh):
    vocab = mesh.shape["vocab"]
    whole = Mesh(
        mesh.devices.reshape(SIDE, SIDE, vocab // SIDE // 2, 2), ("group", "x", "z", "core")
    )
    placed = (
        P("group", VOCAB_AXES),
        P(),
        P("group", VOCAB_AXES),
        P(VOCAB_AXES, None, None, None),
        P(VOCAB_AXES, None, None, None),
        P(VOCAB_AXES, "group"),
        P(),
        P(),
        P(VOCAB_AXES, None),
        P(VOCAB_AXES, None),
        P(),
    )
    return jax.shard_map(
        per_device,
        mesh=whole,
        in_specs=placed,
        out_specs=(P("group", VOCAB_AXES), P("group", VOCAB_AXES)),
        check_vma=False,
    )
```
